256 devices in a mesh: dp: 32 (over z, x), row: 2 (over core), col: 4 (over y).
Axes of the slice: x: 4, y: 4, z: 8, core: 2. Of those that a mesh axis runs over, the one named last changes fastest.
Arguments:
- weight: float32 [256, 24576], P(('row', 'dp'), 'col'), may hold values from -36 to 36, as said below
- momentum: float32 [256, 24576], P(('row', 'dp'), 'col'), may hold values from -1.5 to 1.5
- grad_parts: bfloat16 [32, 256, 24576], P('dp', 'row', 'col'), may hold values from -1.8 to 1.8, as said below
Outputs:
- new_weight: float32 [256, 24576], P(('row', 'dp'), 'col')
- new_momentum: float32 [256, 24576], P(('row', 'dp'), 'col')
The draws below stay inside these ranges and needn't reach their ends.
Inputs may be any that keep to these rules, and one draw needn't show every extreme that they name: `weight`: entries of the matrix, finite. `grad_parts`: entries of the partials, finite.
All inputs are finite; a program needn't handle non-finite values.
Results may differ from the reference program's by a relative error of at most 0.0003.
Values sent between devices are 32-bit elements; how exact they have to be, the bound alone decides.
No kernel may reach another device: no remote copies, remote signals or barrier semaphores. Data moves between devices by JAX's collectives and lax.ppermute only.
A program may use at most 64 MiB of HBM per device.

```python
import math
import jax
import jax.numpy as jnp
from jax import lax

COLS = 24576
ROWS = 256
N_DP = 32


def draw_weight(key, part):
    key = jax.random.fold_in(key, 1)
    first, second, third = jax.random.split(key, 3)
    row_scale = jnp.exp(jax.random.uniform(first, (ROWS, 1), jnp.float32, math.log(0.3), math.log(3.0)))
    col_scale = jnp.exp(jax.random.uniform(second, (1, COLS), jnp.float32, math.log(0.5), math.log(2.0)))
    noise = jnp.clip(jax.random.normal(third, (ROWS, COLS), jnp.float32), -6.0, 6.0)
    return noise * row_scale * col_scale


def draw_grad_parts(key, part):
    key = jax.random.fold_in(key, 2)
    first = jax.random.fold_in(key, 0)
    second = jax.random.fold_in(key, 1)
    fourth = jax.random.fold_in(key, 3)
    row_scale = jnp.exp(jax.random.uniform(first, (1, ROWS, 1), jnp.float32, math.log(0.001), math.log(0.1)))
    rising = jnp.exp(math.log(3.0) * jnp.arange(COLS, dtype=jnp.float32) / COLS)
    col_scale = rising * jnp.exp(jax.random.uniform(second, (COLS,), jnp.float32, math.log(0.5), math.log(5.0)))
    col_scale = col_scale.reshape(1, 1, COLS) / 5.0
    noise = jnp.clip(jax.random.normal(fourth, (N_DP, ROWS, COLS), jnp.float32), -6.0, 6.0)
    return (noise * row_scale * col_scale).astype(jnp.bfloat16)


def block_levels(rng, extent, pieces, smallest, high):
    def one(position, parts):
        steps = jax.random.uniform(jax.random.fold_in(jax.random.fold_in(rng, 6), position), (parts,), jnp.float32, smallest / len(pieces), high / len(pieces))
        return jnp.repeat(jnp.exp(steps), extent[position] // parts).reshape((-1,) + (1,) * (len(extent) - position - 1))

    factor_of = one(*pieces[0])
    for cut in pieces[1:]:
        factor_of = factor_of * one(*cut)
    return factor_of


def normal_values(own_key, dims, scale, bound, cuts=(), held_as=jnp.bfloat16):
    factor_of = block_levels(own_key, dims, cuts, -0.22, 0.18) if cuts else 1.0
    result = jax.random.normal(own_key, dims, jnp.float32) * scale * factor_of
    return jnp.minimum(jnp.maximum(result, -bound), bound).astype(held_as)


def setup_inputs(seed: int = 0) -> dict:
    seeds = jax.random.split(jax.random.key(seed), 4)
    weight = draw_weight(jax.random.fold_in(seeds[3], 71), 0)
    momentum = normal_values(seeds[1], (ROWS, COLS), 0.1, 1.5, ((0, 64), (1, 4)), jnp.float32)
    grad_parts = draw_grad_parts(jax.random.fold_in(seeds[3], 71), 0)
    return {"weight": weight, "momentum": momentum, "grad_parts": grad_parts}


clip_bound = 0.08
small_term = 1e-06
momentum_decay = 0.9
learn_rate = 1.0

def apply_update(weight, momentum, gradient, weight_sq, grad_sq):
    factor = jnp.minimum(1.0, clip_bound * jnp.sqrt(weight_sq) * lax.rsqrt(grad_sq + small_term))
    new_momentum = momentum_decay * momentum + factor[:, None] * gradient
    return (weight - learn_rate * new_momentum, new_momentum)

def reference(weight, momentum, grad_parts):
    gradient = jnp.zeros(weight.shape, jnp.float32)
    for member in range(N_DP):
        gradient = gradient + grad_parts[member].astype(jnp.float32)
    weight_sq = lax.optimization_barrier(jnp.sum(weight * weight, axis=1))
    grad_sq = lax.optimization_barrier(jnp.sum(gradient * gradient, axis=1))
    new_weight, new_momentum = apply_update(weight, momentum, gradient, weight_sq, grad_sq)
    return (new_weight, new_momentum)
```

```python
import jax
import jax.numpy as jnp
from jax import lax
from jax.sharding import PartitionSpec as P

clip_bound = 0.08
small_term = 1e-06
momentum_decay = 0.9
learn_rate = 1.0

NZ, NX, NY, NCORE = 8, 4, 4, 2
SPLIT = 3072


def pairs_zx(target):
    out = []
    for z in range(NZ):
        for x in range(NX):
            for core in range(NCORE):
                tz, tx = target(z, x, core)
                out.append((((z * NX + x) * NCORE + core), ((tz % NZ) * NX + tx) * NCORE + core))
    return out


def sign(z, core):
    return 2 * ((z + core) % 2) - 1


def x_first(core):
    return 1 + 2 * core


def x_second(core):
    return 3 - 2 * core


def send(value, target):
    return lax.ppermute(value, ("dp", "row"), pairs_zx(target))


def send_x_first(value):
    return send(value, lambda z, x, core: (z, x ^ x_first(core)))


def send_x_second(value):
    return send(value, lambda z, x, core: (z, x ^ x_second(core)))


def send_z_pair(value):
    return send(value, lambda z, x, core: (z - sign(z, core), x))


def send_z_far(value, k):
    return send(value, lambda z, x, core: (z + sign(z, core) * k, x))


def pick(value, index, axis):
    return lax.dynamic_index_in_dim(value, index, axis, keepdims=False)


def sum_parts(local):
    cols = local.shape[1]
    cut = min(SPLIT, cols // 2)
    dp = lax.axis_index("dp")
    core = lax.axis_index("row")
    z, x = dp // NX, dp % NX
    s = 2 * ((z + core) % 2) - 1
    m1, m2, diag = x ^ (1 + 2 * core), x ^ (3 - 2 * core), x ^ 2
    keep_z = [(z + s * k + NZ) % NZ for k in range(4)]
    give_z = [(z - s * (1 + k) + NZ) % NZ for k in range(4)]

    f32 = jnp.float32
    a = local[:, :cut].reshape(NZ, NX, 4, cut)
    b = local[:, cut:].reshape(NZ, NX, 4, cols - cut)

    a_got = send_x_first(jnp.stack([pick(a, m1, 1), pick(a, diag, 1)]).astype(f32))
    b_got = send_z_pair(jnp.stack([pick(b, i, 0) for i in give_z]).astype(f32))
    a_out = pick(a, m2, 1).astype(f32) + a_got[1]
    a_got2 = send_x_second(a_out)
    b_sum = jnp.stack([pick(b, i, 0) for i in keep_z]).astype(f32) + b_got
    b_got2 = send_x_first(jnp.stack([pick(b_sum, m1, 1), pick(b_sum, diag, 1)]))
    a_sum = pick(a, x, 1).astype(f32) + a_got[0] + a_got2
    a_got3 = send_z_pair(jnp.stack([pick(a_sum, i, 0) for i in give_z]))
    b_got3 = send_x_second(pick(b_sum, m2, 1) + b_got2[1])
    a_sum = jnp.stack([pick(a_sum, i, 0) for i in keep_z]) + a_got3
    b_sum = pick(b_sum, x, 1) + b_got2[0] + b_got3
    far = [send_z_far(jnp.concatenate([a_sum[k], b_sum[k]], axis=1), k) for k in (1, 2, 3)]
    return jnp.concatenate([a_sum[0], b_sum[0]], axis=1) + far[0] + far[1] + far[2]


def sum_over_col(value):
    value = value + lax.ppermute(value, "col", [(i, i ^ 1) for i in range(NY)])
    return value + lax.ppermute(value, "col", [(i, i ^ 3) for i in range(NY)])


def per_device(weight, momentum, grad_parts):
    weight_sq = sum_over_col(jnp.sum(weight * weight, axis=1, keepdims=True))
    gradient = sum_parts(grad_parts[0])
    grad_sq = sum_over_col(jnp.sum(gradient * gradient, axis=1, keepdims=True))
    factor = jnp.minimum(1.0, clip_bound * jnp.sqrt(weight_sq) * lax.rsqrt(grad_sq + small_term))
    new_momentum = momentum_decay * momentum + factor * gradient
    return (weight - learn_rate * new_momentum, new_momentum)


def solution(mesh):
    in_specs = (P(("row", "dp"), "col"), P(("row", "dp"), "col"), P("dp", "row", "col"))
    out_specs = (P(("row", "dp"), "col"), P(("row", "dp"), "col"))
    return jax.shard_map(
        per_device, mesh=mesh, in_specs=in_specs, out_specs=out_specs, check_vma=False
    )
```

```python
import functools

import jax
import jax.numpy as jnp
from jax import lax
from jax.experimental import pallas as pl
from jax.experimental.pallas import tpu as pltpu
from jax.sharding import PartitionSpec as P

clip_bound = 0.08
small_term = 1e-06
momentum_decay = 0.9
learn_rate = 1.0

NZ, NX, NY, NCORE = 8, 4, 4, 2
SHARE, TOTAL = 1, 2
CHUNK = 512
ORDER = (1, 2, 3)
COL_ORDER = (1, 3, 2)


def pairs_zx(target):
    out = []
    for z in range(NZ):
        for x in range(NX):
            for core in range(NCORE):
                tz, tx = target(z, x, core)
                out.append((((z * NX + x) * NCORE + core), ((tz % NZ) * NX + tx) * NCORE + core))
    return out


def sign(z, core):
    return 2 * ((z + core) % 2) - 1


def send(value, target):
    return lax.ppermute(value, ("dp", "row"), pairs_zx(target))


def send_x_first(value):
    return send(value, lambda z, x, core: (z, x ^ (1 + 2 * core)))


def send_x_second(value):
    return send(value, lambda z, x, core: (z, x ^ (3 - 2 * core)))


def send_z_pair(value):
    return send(value, lambda z, x, core: (z - sign(z, core), x))


def send_z_far(value, k):
    return send(value, lambda z, x, core: (z + sign(z, core) * k, x))


def pick(value, index, axis):
    return lax.dynamic_index_in_dim(value, index, axis, keepdims=False)


def place():
    dp, core = lax.axis_index("dp"), lax.axis_index("row")
    z, x = lax.div(dp, NX), lax.rem(dp, NX)
    return z, x, core, 2 * lax.rem(z + core, 2) - 1


def x_high(x, core):
    h = lax.broadcasted_iota(jnp.int32, (8, 1), 0) // 4
    return (lax.div(x, 2) ^ jnp.where((h != lax.rem(x, 2)) & (core == 0), 1, 0)) == 1


def z_high(z, s, j):
    return (z + s * (((j - z) * s) & 3)) & 7 >= 4


def each_chunk(cols, body):
    n = CHUNK if cols % CHUNK == 0 else 128
    lax.fori_loop(0, cols // n, lambda i, c: (body(pl.multiple_of(i * n, n), n), c)[1], 0)


def give_z_kernel(cut, src, out, buf, sem):
    z, x, core, s = place()
    copies = []
    for j in range(4):
        row = pl.multiple_of(jnp.where(z_high(z, s, j), 0, 64) + j * 16, 16)
        copies.append(pltpu.make_async_copy(src.at[pl.ds(row, 16), pl.ds(cut, buf.shape[2])], buf.at[j], sem.at[j]))
    for copy in copies:
        copy.start()
    for copy in copies:
        copy.wait()

    def body(first, n):
        for j in range(4):
            here = (j, slice(None), pl.ds(first, n))
            out[here] = buf[here].astype(jnp.float32)

    each_chunk(buf.shape[2], body)


def give_x_kernel(cut, src, out, buf, sem):
    z, x, core, s = place()
    copies = [
        pltpu.make_async_copy(src.at[pl.ds(j * 32, 32), pl.ds(0, cut)], buf.at[j], sem.at[j]) for j in range(4)
    ]
    for copy in copies:
        copy.start()
    for copy in copies:
        copy.wait()

    def body(first, n):
        high = jnp.broadcast_to(jnp.where(x_high(x, core), 1, 0), (8, n)) == 0
        for k in range(NZ):
            rows = buf[k // 2, k % 2 * 16 : k % 2 * 16 + 16, pl.ds(first, n)].astype(jnp.float32)
            out[k, :, pl.ds(first, n)] = jnp.where(high, rows[8:], rows[:8])

    each_chunk(cut, body)


def b_kernel(cut, src, got, own, out, buf, sem):
    z, x, core, s = place()
    copies = []
    for j in range(4):
        row = pl.multiple_of(jnp.where(z_high(z, s, j), 64, 0) + j * 16, 16)
        copies.append(pltpu.make_async_copy(src.at[pl.ds(row, 16), pl.ds(cut, buf.shape[2])], buf.at[j], sem.at[j]))
    for copy in copies:
        copy.start()
    for copy in copies:
        copy.wait()

    def body(first, n):
        cols = pl.ds(first, n)
        high = jnp.broadcast_to(jnp.where(x_high(x, core), 1, 0), (8, n)) == 1
        for j in range(4):
            rows = buf[j, :, cols].astype(jnp.float32) + got[j, :, cols]
            own[j * 8 : j * 8 + 8, cols] = jnp.where(high, rows[8:], rows[:8])
            out[j * 8 : j * 8 + 8, cols] = jnp.where(high, rows[:8], rows[8:])

    each_chunk(buf.shape[2], body)


def a_kernel(cut, src, got, own, out, buf, sem):
    z, x, core, s = place()
    copies = [
        pltpu.make_async_copy(src.at[pl.ds(j * 32, 32), pl.ds(0, cut)], buf.at[j], sem.at[j]) for j in range(4)
    ]
    for copy in copies:
        copy.start()
    for copy in copies:
        copy.wait()

    def body(first, n):
        cols = pl.ds(first, n)
        high = jnp.broadcast_to(jnp.where(x_high(x, core), 1, 0), (8, n)) == 1
        for j in range(4):
            there = []
            for zz in (j, j + 4):
                rows = buf[zz // 2, zz % 2 * 16 : zz % 2 * 16 + 16, cols].astype(jnp.float32)
                there.append(jnp.where(high, rows[8:], rows[:8]) + got[zz, :, cols])
            second = z_high(z, s, j)
            own[j * 8 : j * 8 + 8, cols] = jnp.where(second, there[1], there[0])
            out[j * 8 : j * 8 + 8, cols] = jnp.where(second, there[0], there[1])

    each_chunk(cut, body)


def call(kernel, outs, scratch, copies, local, *got):
    got = [pltpu.with_memory_space_constraint(v, pltpu.VMEM) for v in got]
    vmem = pl.BlockSpec(memory_space=pltpu.VMEM)
    return pl.pallas_call(
        kernel,
        in_specs=[pl.BlockSpec(memory_space=pl.ANY)] + [vmem] * len(got),
        out_specs=[vmem] * len(outs),
        out_shape=[pltpu.VMEM(shape, jnp.float32) for shape in outs],
        scratch_shapes=[pltpu.VMEM(shape, jnp.bfloat16) for shape in scratch] + [pltpu.SemaphoreType.DMA((copies,))],
        compiler_params=pltpu.CompilerParams(vmem_limit_bytes=4 << 20),
        cost_estimate=pl.CostEstimate(flops=1 << 18, bytes_accessed=1 << 20, transcendentals=0),
    )(local, *got)


def sum_parts(local):
    cols = local.shape[1]
    cut = cols * SHARE // TOTAL
    rest = cols - cut
    z, x, core, s = place()
    odd = lax.rem(x, 2) == 1

    (b_out,) = call(functools.partial(give_z_kernel, cut), [(4, 16, rest)], [(4, 16, rest)], 4, local)
    b_got = send_z_pair(b_out)
    later = lax.optimization_barrier((local, b_out))[0]
    (a_out,) = call(functools.partial(give_x_kernel, cut), [(NZ, 8, cut)], [(4, 32, cut)], 4, later)
    a_got = send_x_first(a_out)
    b_own, b_out = call(functools.partial(b_kernel, cut), [(32, rest)] * 2, [(4, 16, rest)], 4, local, b_got)
    b_got = send_x_first(b_out)
    later = lax.optimization_barrier((local, b_out))[0]
    a_own, a_out = call(functools.partial(a_kernel, cut), [(32, cut)] * 2, [(4, 32, cut)], 4, later, a_got)
    a_got = send_z_pair(a_out)
    own = jnp.concatenate([a_own + a_got, b_own + b_got], axis=1).reshape(4, 8, cols)
    own, out = jnp.where(odd, own[:, 4:], own[:, :4]), jnp.where(odd, own[:, :4], own[:, 4:])
    own = own + send_x_second(out)
    far = [send_z_far(pick(own, (z + s * k) & 3, 0), k) for k in ORDER]
    return pick(own, z & 3, 0) + far[0] + far[1] + far[2]


def sum_over_col(value):
    got = [lax.ppermute(value, "col", [(i, i ^ m) for i in range(NY)]) for m in COL_ORDER]
    return value + got[0] + got[1] + got[2]


def per_device(weight, momentum, grad_parts):
    gradient = sum_parts(grad_parts[0])
    squares = [jnp.sum(v * v, axis=1, keepdims=True) for v in (weight, gradient)]
    squares = sum_over_col(jnp.concatenate(squares, axis=1))
    weight_sq, grad_sq = squares[:, :1], squares[:, 1:]
    factor = jnp.minimum(1.0, clip_bound * jnp.sqrt(weight_sq) * lax.rsqrt(grad_sq + small_term))
    new_momentum = momentum_decay * momentum + factor * gradient
    return (weight - learn_rate * new_momentum, new_momentum)


def solution(mesh):
    in_specs = (P(("row", "dp"), "col"), P(("row", "dp"), "col"), P("dp", "row", "col"))
    out_specs = (P(("row", "dp"), "col"), P(("row", "dp"), "col"))
    return jax.shard_map(
        per_device, mesh=mesh, in_specs=in_specs, out_specs=out_specs, check_vma=False
    )
```

```python
import functools

import jax
import jax.numpy as jnp
from jax import lax
from jax.experimental import pallas as pl
from jax.experimental.pallas import tpu as pltpu
from jax.sharding import PartitionSpec as P

clip_bound = 0.08
small_term = 1e-06
momentum_decay = 0.9
learn_rate = 1.0

NZ, NX, NY, NCORE = 8, 4, 4, 2
PIECES = 3
LIMIT = 2 << 20
CHUNK = 512
ORDER = (3, 2, 1)
COL_ORDER = (1, 3, 2)


def pairs_zx(target):
    out = []
    for z in range(NZ):
        for x in range(NX):
            for core in range(NCORE):
                tz, tx = target(z, x, core)
                out.append((((z * NX + x) * NCORE + core), ((tz % NZ) * NX + tx) * NCORE + core))
    return out


def sign(z, core):
    return 2 * ((z + core) % 2) - 1


def send(value, target):
    return lax.ppermute(value, ("dp", "row"), pairs_zx(target))


def send_x_first(value):
    return send(value, lambda z, x, core: (z, x ^ (1 + 2 * core)))


def send_x_second(value):
    return send(value, lambda z, x, core: (z, x ^ (3 - 2 * core)))


def send_z_pair(value):
    return send(value, lambda z, x, core: (z - sign(z, core), x))


def send_z_far(value, k):
    return send(value, lambda z, x, core: (z + sign(z, core) * k, x))


def pick(value, index, axis):
    return lax.dynamic_index_in_dim(value, index, axis, keepdims=False)


def after(value, other):
    return lax.optimization_barrier((value, other))[0]


def place():
    dp, core = lax.axis_index("dp"), lax.axis_index("row")
    z, x = lax.div(dp, NX), lax.rem(dp, NX)
    return z, x, core, 2 * lax.rem(z + core, 2) - 1


def x_high(x, core):
    h = lax.broadcasted_iota(jnp.int32, (8, 1), 0) // 4
    return (lax.div(x, 2) ^ jnp.where((h != lax.rem(x, 2)) & (core == 0), 1, 0)) == 1


def z_high(z, s, j):
    return (z + s * (((j - z) * s) & 3)) & 7 >= 4


def each_chunk(cols, body):
    n = CHUNK if cols % CHUNK == 0 else 128
    lax.fori_loop(0, cols // n, lambda i, c: (body(pl.multiple_of(i * n, n), n), c)[1], 0)


def give_z_kernel(start, src, out, buf, sem):
    z, x, core, s = place()
    copies = []
    for j in range(4):
        row = pl.multiple_of(jnp.where(z_high(z, s, j), 0, 64) + j * 16, 16)
        copies.append(pltpu.make_async_copy(src.at[pl.ds(row, 16), pl.ds(start, buf.shape[2])], buf.at[j], sem.at[j]))
    for copy in copies:
        copy.start()
    for copy in copies:
        copy.wait()

    def body(first, n):
        for j in range(4):
            here = (j, slice(None), pl.ds(first, n))
            out[here] = buf[here].astype(jnp.float32)

    each_chunk(buf.shape[2], body)


def give_x_kernel(start, src, out, buf, sem):
    z, x, core, s = place()
    copies = [
        pltpu.make_async_copy(src.at[pl.ds(j * 32, 32), pl.ds(start, buf.shape[2])], buf.at[j], sem.at[j]) for j in range(4)
    ]
    for copy in copies:
        copy.start()
    for copy in copies:
        copy.wait()

    def body(first, n):
        high = jnp.broadcast_to(jnp.where(x_high(x, core), 1, 0), (8, n)) == 0
        for k in range(NZ):
            rows = buf[k // 2, k % 2 * 16 : k % 2 * 16 + 16, pl.ds(first, n)].astype(jnp.float32)
            out[k, :, pl.ds(first, n)] = jnp.where(high, rows[8:], rows[:8])

    each_chunk(buf.shape[2], body)


def b_kernel(start, src, got, own, out, buf, sem):
    z, x, core, s = place()
    copies = []
    for j in range(4):
        row = pl.multiple_of(jnp.where(z_high(z, s, j), 64, 0) + j * 16, 16)
        copies.append(pltpu.make_async_copy(src.at[pl.ds(row, 16), pl.ds(start, buf.shape[2])], buf.at[j], sem.at[j]))
    for copy in copies:
        copy.start()
    for copy in copies:
        copy.wait()

    def body(first, n):
        cols = pl.ds(first, n)
        high = jnp.broadcast_to(jnp.where(x_high(x, core), 1, 0), (8, n)) == 1
        for j in range(4):
            rows = buf[j, :, cols].astype(jnp.float32) + got[j, :, cols]
            own[j * 8 : j * 8 + 8, cols] = jnp.where(high, rows[8:], rows[:8])
            out[j * 8 : j * 8 + 8, cols] = jnp.where(high, rows[:8], rows[8:])

    each_chunk(buf.shape[2], body)


def a_kernel(start, src, got, own, out, buf, sem):
    z, x, core, s = place()
    copies = [
        pltpu.make_async_copy(src.at[pl.ds(j * 32, 32), pl.ds(start, buf.shape[2])], buf.at[j], sem.at[j]) for j in range(4)
    ]
    for copy in copies:
        copy.start()
    for copy in copies:
        copy.wait()

    def body(first, n):
        cols = pl.ds(first, n)
        high = jnp.broadcast_to(jnp.where(x_high(x, core), 1, 0), (8, n)) == 1
        for j in range(4):
            there = []
            for zz in (j, j + 4):
                rows = buf[zz // 2, zz % 2 * 16 : zz % 2 * 16 + 16, cols].astype(jnp.float32)
                there.append(jnp.where(high, rows[8:], rows[:8]) + got[zz, :, cols])
            second = z_high(z, s, j)
            own[j * 8 : j * 8 + 8, cols] = jnp.where(second, there[1], there[0])
            out[j * 8 : j * 8 + 8, cols] = jnp.where(second, there[0], there[1])

    each_chunk(buf.shape[2], body)


def join_kernel(a, a_got, b, b_got, own, out):
    z, x, core, s = place()
    odd = lax.rem(x, 2) == 1

    def body(first, n):
        top = lax.broadcasted_iota(jnp.int32, (8, n), 0) < 4
        for kept, got, start in ((b, b_got, a.shape[1]), (a, a_got, 0)):
            for j in range(2):
                there = []
                for i in range(2):
                    here = (slice((2 * j + i) * 8, (2 * j + i) * 8 + 8), pl.ds(first, n))
                    rows = kept[here] + got[here]
                    turned = jnp.concatenate([rows[4:], rows[:4]], axis=0)
                    there.append((jnp.where(odd, turned, rows), jnp.where(odd, rows, turned)))
                here = (slice(j * 8, j * 8 + 8), pl.ds(start + first, n))
                own[here] = jnp.where(top, there[0][0], there[1][1])
                out[here] = jnp.where(top, there[0][1], there[1][0])

    each_chunk(a.shape[1], body)


def call(kernel, outs, scratch, *args):
    vmem = pl.BlockSpec(memory_space=pltpu.VMEM)
    specs = [vmem] * len(args)
    if scratch:
        specs[0] = pl.BlockSpec(memory_space=pl.ANY)
    args = [v if spec is not vmem else pltpu.with_memory_space_constraint(v, pltpu.VMEM) for v, spec in zip(args, specs)]
    return pl.pallas_call(
        kernel,
        in_specs=specs,
        out_specs=[vmem] * len(outs),
        out_shape=[pltpu.VMEM(shape, jnp.float32) for shape in outs],
        scratch_shapes=[pltpu.VMEM(scratch, jnp.bfloat16), pltpu.SemaphoreType.DMA((scratch[0],))] if scratch else [],
        compiler_params=pltpu.CompilerParams(vmem_limit_bytes=LIMIT),
        cost_estimate=pl.CostEstimate(flops=1024, bytes_accessed=1024, transcendentals=0),
    )(*args)


def last_step(own, z, s):
    out, last = [], None
    for k in ORDER:
        part = pick(own, (z + s * k) & 3, 0)
        out.append(part if last is None else after(part, last))
        last = out[-1]
    total = pick(own, z & 3, 0)
    for part, k in zip(out, ORDER):
        total = total + send_z_far(part, k)
    return total


def sum_parts(local):
    cols = local.shape[1]
    n = cols // (2 * PIECES)
    a_at, b_at = [2 * i * n for i in range(PIECES)], [(2 * i + 1) * n for i in range(PIECES)]
    z, x, core, s = place()
    odd = lax.rem(x, 2) == 1

    later, a_got, b_got = local, [], []
    for a, b in zip(a_at, b_at):
        (out,) = call(functools.partial(give_z_kernel, b), [(4, 16, n)], (4, 16, n), later)
        b_got.append(send_z_pair(out))
        later = after(local, out)
        (out,) = call(functools.partial(give_x_kernel, a), [(NZ, 8, n)], (4, 32, n), later)
        a_got.append(send_x_first(out))
        later = after(local, out)
    a_own, b_own = [], []
    for i in range(PIECES):
        own, out = call(functools.partial(b_kernel, b_at[i]), [(32, n)] * 2, (4, 16, n), later, b_got[i])
        b_own.append((own, send_x_first(out)))
        later = after(local, out)
        own, out = call(functools.partial(a_kernel, a_at[i]), [(32, n)] * 2, (4, 32, n), later, a_got[i])
        a_own.append((own, send_z_pair(out)))
        later = after(local, out)
    kept, last = [], None
    for (a, a_got), (b, b_got) in zip(a_own, b_own):
        own, out = call(join_kernel, [(16, 2 * n)] * 2, None, a if last is None else after(a, last), a_got, b, b_got)
        kept.append((own, send_x_second(out)))
        last = out
    done = []
    for own, got in kept:
        done.append((after(own, done[-1]) if done else own) + got)
    return last_step(jnp.concatenate(done, axis=1).reshape(4, 4, cols), z, s)


def sum_over_col(value):
    got = [lax.ppermute(value, "col", [(i, i ^ m) for i in range(NY)]) for m in COL_ORDER]
    return value + got[0] + got[1] + got[2]


def per_device(weight, momentum, grad_parts):
    gradient = sum_parts(grad_parts[0])
    squares = [jnp.sum(v * v, axis=1, keepdims=True) for v in (weight, gradient)]
    squares = sum_over_col(jnp.concatenate(squares, axis=1))
    weight_sq, grad_sq = squares[:, :1], squares[:, 1:]
    factor = jnp.minimum(1.0, clip_bound * jnp.sqrt(weight_sq) * lax.rsqrt(grad_sq + small_term))
    new_momentum = momentum_decay * momentum + factor * gradient
    return (weight - learn_rate * new_momentum, new_momentum)


def solution(mesh):
    in_specs = (P(("row", "dp"), "col"), P(("row", "dp"), "col"), P("dp", "row", "col"))
    out_specs = (P(("row", "dp"), "col"), P(("row", "dp"), "col"))
    return jax.shard_map(
        per_device, mesh=mesh, in_specs=in_specs, out_specs=out_specs, check_vma=False
    )
```

```python
import functools

import jax
import jax.numpy as jnp
from jax import lax
from jax.experimental import pallas as pl
from jax.experimental.pallas import tpu as pltpu
from jax.sharding import PartitionSpec as P

clip_bound = 0.08
small_term = 1e-06
momentum_decay = 0.9
learn_rate = 1.0

NZ, NX, NY, NCORE = 8, 4, 4, 2
WIDTHS = (1920, 1152)
UNIT = 3072
LIMIT = 2 << 20
CHUNK = 384
ORDER = (3, 2, 1)
COL_ORDER = (1, 3, 2)


def pairs_zx(target):
    out = []
    for z in range(NZ):
        for x in range(NX):
            for core in range(NCORE):
                tz, tx = target(z, x, core)
                out.append((((z * NX + x) * NCORE + core), ((tz % NZ) * NX + tx) * NCORE + core))
    return out


def sign(z, core):
    return 2 * ((z + core) % 2) - 1


def send(value, target):
    return lax.ppermute(value, ("dp", "row"), pairs_zx(target))


def send_x_first(value):
    return send(value, lambda z, x, core: (z, x ^ (1 + 2 * core)))


def send_x_second(value):
    return send(value, lambda z, x, core: (z, x ^ (3 - 2 * core)))


def send_z_pair(value):
    return send(value, lambda z, x, core: (z - sign(z, core), x))


def send_z_far(value, k):
    return send(value, lambda z, x, core: (z + sign(z, core) * k, x))


def pick(value, index, axis):
    return lax.dynamic_index_in_dim(value, index, axis, keepdims=False)


def after(value, other):
    return lax.optimization_barrier((value, other))[0]


def place():
    dp, core = lax.axis_index("dp"), lax.axis_index("row")
    z, x = lax.div(dp, NX), lax.rem(dp, NX)
    return z, x, core, 2 * lax.rem(z + core, 2) - 1


def x_high(x, core):
    h = lax.broadcasted_iota(jnp.int32, (8, 1), 0) // 4
    return (lax.div(x, 2) ^ jnp.where((h != lax.rem(x, 2)) & (core == 0), 1, 0)) == 1


def z_high(z, s, j):
    return (z + s * (((j - z) * s) & 3)) & 7 >= 4


def each_chunk(cols, body):
    n = CHUNK if cols % CHUNK == 0 else 128
    lax.fori_loop(0, cols // n, lambda i, c: (body(pl.multiple_of(i * n, n), n), c)[1], 0)


def give_z_kernel(start, src, out, buf, sem):
    z, x, core, s = place()
    copies = []
    for j in range(4):
        row = pl.multiple_of(jnp.where(z_high(z, s, j), 0, 64) + j * 16, 16)
        copies.append(pltpu.make_async_copy(src.at[pl.ds(row, 16), pl.ds(start, buf.shape[2])], buf.at[j], sem.at[j]))
    for copy in copies:
        copy.start()
    for copy in copies:
        copy.wait()

    def body(first, n):
        for j in range(4):
            here = (j, slice(None), pl.ds(first, n))
            out[here] = buf[here].astype(jnp.float32)

    each_chunk(buf.shape[2], body)


def give_x_kernel(start, src, out, buf, sem):
    z, x, core, s = place()
    copies = [
        pltpu.make_async_copy(src.at[pl.ds(j * 32, 32), pl.ds(start, buf.shape[2])], buf.at[j], sem.at[j]) for j in range(4)
    ]
    for copy in copies:
        copy.start()
    for copy in copies:
        copy.wait()

    def body(first, n):
        high = jnp.broadcast_to(jnp.where(x_high(x, core), 1, 0), (8, n)) == 0
        for k in range(NZ):
            rows = buf[k // 2, k % 2 * 16 : k % 2 * 16 + 16, pl.ds(first, n)].astype(jnp.float32)
            out[k, :, pl.ds(first, n)] = jnp.where(high, rows[8:], rows[:8])

    each_chunk(buf.shape[2], body)


def b_kernel(start, src, got, own, out, buf, sem):
    z, x, core, s = place()
    copies = []
    for j in range(4):
        row = pl.multiple_of(jnp.where(z_high(z, s, j), 64, 0) + j * 16, 16)
        copies.append(pltpu.make_async_copy(src.at[pl.ds(row, 16), pl.ds(start, buf.shape[2])], buf.at[j], sem.at[j]))
    for copy in copies:
        copy.start()
    for copy in copies:
        copy.wait()

    def body(first, n):
        cols = pl.ds(first, n)
        high = jnp.broadcast_to(jnp.where(x_high(x, core), 1, 0), (8, n)) == 1
        for j in range(4):
            rows = buf[j, :, cols].astype(jnp.float32) + got[j, :, cols]
            own[j * 8 : j * 8 + 8, cols] = jnp.where(high, rows[8:], rows[:8])
            out[j * 8 : j * 8 + 8, cols] = jnp.where(high, rows[:8], rows[8:])

    each_chunk(buf.shape[2], body)


def a_kernel(start, src, got, own, out, buf, sem):
    z, x, core, s = place()
    copies = [
        pltpu.make_async_copy(src.at[pl.ds(j * 32, 32), pl.ds(start, buf.shape[2])], buf.at[j], sem.at[j]) for j in range(4)
    ]
    for copy in copies:
        copy.start()
    for copy in copies:
        copy.wait()

    def body(first, n):
        cols = pl.ds(first, n)
        high = jnp.broadcast_to(jnp.where(x_high(x, core), 1, 0), (8, n)) == 1
        for j in range(4):
            there = []
            for zz in (j, j + 4):
                rows = buf[zz // 2, zz % 2 * 16 : zz % 2 * 16 + 16, cols].astype(jnp.float32)
                there.append(jnp.where(high, rows[8:], rows[:8]) + got[zz, :, cols])
            second = z_high(z, s, j)
            own[j * 8 : j * 8 + 8, cols] = jnp.where(second, there[1], there[0])
            out[j * 8 : j * 8 + 8, cols] = jnp.where(second, there[0], there[1])

    each_chunk(buf.shape[2], body)


def join_kernel(a, a_got, b, b_got, own, out):
    z, x, core, s = place()
    odd = lax.rem(x, 2) == 1

    def body(first, n):
        top = lax.broadcasted_iota(jnp.int32, (8, n), 0) < 4
        for kept, got, start in ((b, b_got, a.shape[1]), (a, a_got, 0)):
            for j in range(2):
                there = []
                for i in range(2):
                    here = (slice((2 * j + i) * 8, (2 * j + i) * 8 + 8), pl.ds(first, n))
                    rows = kept[here] + got[here]
                    turned = jnp.concatenate([rows[4:], rows[:4]], axis=0)
                    there.append((jnp.where(odd, turned, rows), jnp.where(odd, rows, turned)))
                here = (slice(j * 8, j * 8 + 8), pl.ds(start + first, n))
                own[here] = jnp.where(top, there[0][0], there[1][1])
                out[here] = jnp.where(top, there[0][1], there[1][0])

    each_chunk(a.shape[1], body)


def call(kernel, outs, scratch, *args, limit=LIMIT):
    vmem = pl.BlockSpec(memory_space=pltpu.VMEM)
    specs = [vmem] * len(args)
    if scratch:
        specs[0] = pl.BlockSpec(memory_space=pl.ANY)
    args = [v if spec is not vmem else pltpu.with_memory_space_constraint(v, pltpu.VMEM) for v, spec in zip(args, specs)]
    return pl.pallas_call(
        kernel,
        in_specs=specs,
        out_specs=[vmem] * len(outs),
        out_shape=[pltpu.VMEM(shape, jnp.float32) for shape in outs],
        scratch_shapes=[pltpu.VMEM(scratch, jnp.bfloat16), pltpu.SemaphoreType.DMA((scratch[0],))] if scratch else [],
        compiler_params=pltpu.CompilerParams(vmem_limit_bytes=limit),
        cost_estimate=pl.CostEstimate(flops=1024, bytes_accessed=1024, transcendentals=0),
    )(*args)


def last_step(own, z, s):
    out, last = [], None
    for k in ORDER:
        part = pick(own, (z + s * k) & 3, 0)
        out.append(part if last is None else after(part, last))
        last = out[-1]
    total = pick(own, z & 3, 0)
    for part, k in zip(out, ORDER):
        total = total + send_z_far(part, k)
    return total


def sum_parts(local):
    cols = local.shape[1]
    widths = [cols // 2 * w // UNIT for w in WIDTHS]
    a_at = [2 * sum(widths[:i]) for i in range(len(widths))]
    b_at = [a + w for a, w in zip(a_at, widths)]
    z, x, core, s = place()
    odd = lax.rem(x, 2) == 1

    later, a_got, b_got = local, [], []
    for a, b, n in zip(a_at, b_at, widths):
        (out,) = call(functools.partial(give_x_kernel, a), [(NZ, 8, n)], (4, 32, n), later, limit=None if later is local else LIMIT)
        a_got.append(send_x_first(out))
        later = after(local, out)
        (out,) = call(functools.partial(give_z_kernel, b), [(4, 16, n)], (4, 16, n), later)
        b_got.append(send_z_pair(out))
        later = after(local, out)
    a_own, b_own = [], []
    for i, n in enumerate(widths):
        own, out = call(functools.partial(a_kernel, a_at[i]), [(32, n)] * 2, (4, 32, n), later, a_got[i])
        a_own.append((own, send_z_pair(out)))
        later = after(local, out)
        own, out = call(functools.partial(b_kernel, b_at[i]), [(32, n)] * 2, (4, 16, n), later, b_got[i])
        b_own.append((own, send_x_first(out)))
        later = after(local, out)
    kept, last = [], None
    for (a, a_got), (b, b_got), n in zip(a_own, b_own, widths):
        own, out = call(join_kernel, [(16, 2 * n)] * 2, None, a if last is None else after(a, last), a_got, b, b_got)
        kept.append((own, send_x_second(out)))
        last = out
    done = []
    for own, got in kept:
        done.append((after(own, done[-1]) if done else own) + got)
    return last_step(jnp.concatenate(done, axis=1).reshape(4, 4, cols), z, s)


def sum_over_col(value):
    got = [lax.ppermute(value, "col", [(i, i ^ m) for i in range(NY)]) for m in COL_ORDER]
    return value + got[0] + got[1] + got[2]


def per_device(weight, momentum, grad_parts):
    gradient = sum_parts(grad_parts[0])
    squares = [jnp.sum(v * v, axis=1, keepdims=True) for v in (weight, gradient)]
    squares = sum_over_col(jnp.concatenate(squares, axis=1))
    weight_sq, grad_sq = squares[:, :1], squares[:, 1:]
    factor = jnp.minimum(1.0, clip_bound * jnp.sqrt(weight_sq) * lax.rsqrt(grad_sq + small_term))
    new_momentum = momentum_decay * momentum + factor * gradient
    return (weight - learn_rate * new_momentum, new_momentum)


def solution(mesh):
    in_specs = (P(("row", "dp"), "col"), P(("row", "dp"), "col"), P("dp", "row", "col"))
    out_specs = (P(("row", "dp"), "col"), P(("row", "dp"), "col"))
    return jax.shard_map(
        per_device, mesh=mesh, in_specs=in_specs, out_specs=out_specs, check_vma=False
    )
```

```python
import functools

import jax
import jax.numpy as jnp
from jax import lax
from jax.experimental import pallas as pl
from jax.experimental.pallas import tpu as pltpu
from jax.sharding import PartitionSpec as P

clip_bound = 0.08
small_term = 1e-06
momentum_decay = 0.9
learn_rate = 1.0

NZ, NX, NY, NCORE = 8, 4, 4, 2
WIDTHS = (1920, 1152)
UNIT = 3072
LIMIT = 2 << 20
CHUNK = 384
ORDER = (3, 2, 1)
COL_ORDER = (1, 3, 2)


def pairs_zx(target):
    out = []
    for z in range(NZ):
        for x in range(NX):
            for core in range(NCORE):
                tz, tx = target(z, x, core)
                out.append((((z * NX + x) * NCORE + core), ((tz % NZ) * NX + tx) * NCORE + core))
    return out


def sign(z, core):
    return 2 * ((z + core) % 2) - 1


def send(value, target):
    return lax.ppermute(value, ("dp", "row"), pairs_zx(target))


def send_x_first(value):
    return send(value, lambda z, x, core: (z, x ^ (1 + 2 * core)))


def send_x_second(value):
    return send(value, lambda z, x, core: (z, x ^ (3 - 2 * core)))


def send_z_pair(value):
    return send(value, lambda z, x, core: (z - sign(z, core), x))


def send_z_far(value, k):
    return send(value, lambda z, x, core: (z + sign(z, core) * k, x))


def pick(value, index, axis):
    return lax.dynamic_index_in_dim(value, index, axis, keepdims=False)


def after(value, other):
    return lax.optimization_barrier((value, other))[0]


def place():
    dp, core = lax.axis_index("dp"), lax.axis_index("row")
    z, x = lax.div(dp, NX), lax.rem(dp, NX)
    return z, x, core, 2 * lax.rem(z + core, 2) - 1


def x_high(x, core):
    h = lax.broadcasted_iota(jnp.int32, (8, 1), 0) // 4
    return (lax.div(x, 2) ^ jnp.where((h != lax.rem(x, 2)) & (core == 0), 1, 0)) == 1


def z_high(z, s, j):
    return (z + s * (((j - z) * s) & 3)) & 7 >= 4


def each_chunk(cols, body):
    n = CHUNK if cols % CHUNK == 0 else 128
    lax.fori_loop(0, cols // n, lambda i, c: (body(pl.multiple_of(i * n, n), n), c)[1], 0)


def give_z_kernel(start, src, out, buf, sem):
    z, x, core, s = place()
    copies = []
    for j in range(4):
        row = pl.multiple_of(jnp.where(z_high(z, s, j), 0, 64) + j * 16, 16)
        copies.append(pltpu.make_async_copy(src.at[pl.ds(row, 16), pl.ds(start, buf.shape[2])], buf.at[j], sem.at[j]))
    for copy in copies:
        copy.start()
    for copy in copies:
        copy.wait()

    def body(first, n):
        for j in range(4):
            here = (j, slice(None), pl.ds(first, n))
            out[here] = buf[here].astype(jnp.float32)

    each_chunk(buf.shape[2], body)


def give_x_kernel(start, src, out, buf, sem):
    z, x, core, s = place()
    copies = [
        pltpu.make_async_copy(src.at[pl.ds(j * 32, 32), pl.ds(start, buf.shape[2])], buf.at[j], sem.at[j]) for j in range(4)
    ]
    for copy in copies:
        copy.start()

    def body(j, first, n):
        high = jnp.broadcast_to(jnp.where(x_high(x, core), 1, 0), (8, n)) == 0
        for k in (2 * j, 2 * j + 1):
            rows = buf[k // 2, k % 2 * 16 : k % 2 * 16 + 16, pl.ds(first, n)].astype(jnp.float32)
            out[k, :, pl.ds(first, n)] = jnp.where(high, rows[8:], rows[:8])

    for j, copy in enumerate(copies):
        copy.wait()
        each_chunk(buf.shape[2], functools.partial(body, j))


def b_kernel(start, src, got, own, out, buf, sem):
    z, x, core, s = place()
    copies = []
    for j in range(4):
        row = pl.multiple_of(jnp.where(z_high(z, s, j), 64, 0) + j * 16, 16)
        copies.append(pltpu.make_async_copy(src.at[pl.ds(row, 16), pl.ds(start, buf.shape[2])], buf.at[j], sem.at[j]))
    for copy in copies:
        copy.start()
    for copy in copies:
        copy.wait()

    def body(first, n):
        cols = pl.ds(first, n)
        high = jnp.broadcast_to(jnp.where(x_high(x, core), 1, 0), (8, n)) == 1
        for j in range(4):
            rows = buf[j, :, cols].astype(jnp.float32) + got[j, :, cols]
            own[j * 8 : j * 8 + 8, cols] = jnp.where(high, rows[8:], rows[:8])
            out[j * 8 : j * 8 + 8, cols] = jnp.where(high, rows[:8], rows[8:])

    each_chunk(buf.shape[2], body)


def a_kernel(start, src, got, own, out, buf, sem):
    z, x, core, s = place()
    copies = [
        pltpu.make_async_copy(src.at[pl.ds(j * 32, 32), pl.ds(start, buf.shape[2])], buf.at[j], sem.at[j]) for j in range(4)
    ]
    for copy in copies:
        copy.start()
    for copy in copies:
        copy.wait()

    def body(first, n):
        cols = pl.ds(first, n)
        high = jnp.broadcast_to(jnp.where(x_high(x, core), 1, 0), (8, n)) == 1
        for j in range(4):
            there = []
            for zz in (j, j + 4):
                rows = buf[zz // 2, zz % 2 * 16 : zz % 2 * 16 + 16, cols].astype(jnp.float32)
                there.append(jnp.where(high, rows[8:], rows[:8]) + got[zz, :, cols])
            second = z_high(z, s, j)
            own[j * 8 : j * 8 + 8, cols] = jnp.where(second, there[1], there[0])
            out[j * 8 : j * 8 + 8, cols] = jnp.where(second, there[0], there[1])

    each_chunk(buf.shape[2], body)


def join_kernel(a, a_got, b, b_got, own, out):
    z, x, core, s = place()
    odd = lax.rem(x, 2) == 1

    def body(first, n):
        top = lax.broadcasted_iota(jnp.int32, (8, n), 0) < 4
        for kept, got, start in ((b, b_got, a.shape[1]), (a, a_got, 0)):
            for j in range(2):
                there = []
                for i in range(2):
                    here = (slice((2 * j + i) * 8, (2 * j + i) * 8 + 8), pl.ds(first, n))
                    rows = kept[here] + got[here]
                    turned = jnp.concatenate([rows[4:], rows[:4]], axis=0)
                    there.append((jnp.where(odd, turned, rows), jnp.where(odd, rows, turned)))
                here = (slice(j * 8, j * 8 + 8), pl.ds(start + first, n))
                own[here] = jnp.where(top, there[0][0], there[1][1])
                out[here] = jnp.where(top, there[0][1], there[1][0])

    each_chunk(a.shape[1], body)


def call(kernel, outs, scratch, *args, limit=LIMIT):
    vmem = pl.BlockSpec(memory_space=pltpu.VMEM)
    specs = [vmem] * len(args)
    if scratch:
        specs[0] = pl.BlockSpec(memory_space=pl.ANY)
    args = [v if spec is not vmem else pltpu.with_memory_space_constraint(v, pltpu.VMEM) for v, spec in zip(args, specs)]
    return pl.pallas_call(
        kernel,
        in_specs=specs,
        out_specs=[vmem] * len(outs),
        out_shape=[pltpu.VMEM(shape, jnp.float32) for shape in outs],
        scratch_shapes=[pltpu.VMEM(scratch, jnp.bfloat16), pltpu.SemaphoreType.DMA((scratch[0],))] if scratch else [],
        compiler_params=pltpu.CompilerParams(vmem_limit_bytes=limit),
        cost_estimate=pl.CostEstimate(flops=1024, bytes_accessed=1024, transcendentals=0),
    )(*args)


def last_step(own, z, s):
    out, last = [], None
    for k in ORDER:
        part = pick(own, (z + s * k) & 3, 0)
        out.append(part if last is None else after(part, last))
        last = out[-1]
    total = pick(own, z & 3, 0)
    for part, k in zip(out, ORDER):
        total = total + send_z_far(part, k)
    return total


def sum_parts(local):
    cols = local.shape[1]
    widths = [cols // 2 * w // UNIT for w in WIDTHS]
    a_at = [2 * sum(widths[:i]) for i in range(len(widths))]
    b_at = [a + w for a, w in zip(a_at, widths)]
    z, x, core, s = place()
    odd = lax.rem(x, 2) == 1

    later, a_got, b_got = local, [], []
    for a, b, n in zip(a_at, b_at, widths):
        (out,) = call(functools.partial(give_x_kernel, a), [(NZ, 8, n)], (4, 32, n), later, limit=None if later is local else LIMIT)
        a_got.append(send_x_first(out))
        later = after(local, out)
        (out,) = call(functools.partial(give_z_kernel, b), [(4, 16, n)], (4, 16, n), later)
        b_got.append(send_z_pair(out))
        later = after(local, out)
    a_own, b_own = [], []
    for i, n in enumerate(widths):
        own, out = call(functools.partial(a_kernel, a_at[i]), [(32, n)] * 2, (4, 32, n), later, a_got[i])
        a_own.append((own, send_z_pair(out)))
        later = after(local, out)
        own, out = call(functools.partial(b_kernel, b_at[i]), [(32, n)] * 2, (4, 16, n), later, b_got[i])
        b_own.append((own, send_x_first(out)))
        later = after(local, out)
    kept, last = [], None
    for (a, a_got), (b, b_got), n in zip(a_own, b_own, widths):
        own, out = call(join_kernel, [(16, 2 * n)] * 2, None, a if last is None else after(a, last), a_got, b, b_got)
        kept.append((own, send_x_second(out)))
        last = out
    done = []
    for own, got in kept:
        done.append((after(own, done[-1]) if done else own) + got)
    return last_step(jnp.concatenate(done, axis=1).reshape(4, 4, cols), z, s)


def sum_over_col(value):
    got = [lax.ppermute(value, "col", [(i, i ^ m) for i in range(NY)]) for m in COL_ORDER]
    return value + got[0] + got[1] + got[2]


def per_device(weight, momentum, grad_parts):
    gradient = sum_parts(grad_parts[0])
    squares = [jnp.sum(v * v, axis=1, keepdims=True) for v in (weight, gradient)]
    squares = sum_over_col(jnp.concatenate(squares, axis=1))
    weight_sq, grad_sq = squares[:, :1], squares[:, 1:]
    factor = jnp.minimum(1.0, clip_bound * jnp.sqrt(weight_sq) * lax.rsqrt(grad_sq + small_term))
    new_momentum = momentum_decay * momentum + factor * gradient
    return (weight - learn_rate * new_momentum, new_momentum)


def solution(mesh):
    in_specs = (P(("row", "dp"), "col"), P(("row", "dp"), "col"), P("dp", "row", "col"))
    out_specs = (P(("row", "dp"), "col"), P(("row", "dp"), "col"))
    return jax.shard_map(
        per_device, mesh=mesh, in_specs=in_specs, out_specs=out_specs, check_vma=False
    )
```

```python
import functools

import jax
import jax.numpy as jnp
from jax import lax
from jax.experimental import pallas as pl
from jax.experimental.pallas import tpu as pltpu
from jax.sharding import PartitionSpec as P

clip_bound = 0.08
small_term = 1e-06
momentum_decay = 0.9
learn_rate = 1.0

NZ, NX, NY, NCORE = 8, 4, 4, 2
WIDTHS = (1920, 1152)
UNIT = 3072
LIMIT = 2 << 20
CHUNK = 384
ORDER = (3, 2, 1)
COL_ORDER = (1, 3, 2)


def pairs_zx(target):
    out = []
    for z in range(NZ):
        for x in range(NX):
            for core in range(NCORE):
                tz, tx = target(z, x, core)
                out.append((((z * NX + x) * NCORE + core), ((tz % NZ) * NX + tx) * NCORE + core))
    return out


def sign(z, core):
    return 2 * ((z + core) % 2) - 1


def send(value, target):
    return lax.ppermute(value, ("dp", "row"), pairs_zx(target))


def send_x_first(value):
    return send(value, lambda z, x, core: (z, x ^ (1 + 2 * core)))


def send_x_second(value):
    return send(value, lambda z, x, core: (z, x ^ (3 - 2 * core)))


def send_z_pair(value):
    return send(value, lambda z, x, core: (z - sign(z, core), x))


def send_z_far(value, k):
    return send(value, lambda z, x, core: (z + sign(z, core) * k, x))


def pick(value, index, axis):
    return lax.dynamic_index_in_dim(value, index, axis, keepdims=False)


def after(value, other):
    return lax.optimization_barrier((value, other))[0]


def place():
    dp, core = lax.axis_index("dp"), lax.axis_index("row")
    z, x = lax.div(dp, NX), lax.rem(dp, NX)
    return z, x, core, 2 * lax.rem(z + core, 2) - 1


def x_high(x, core):
    h = lax.broadcasted_iota(jnp.int32, (8, 1), 0) // 4
    return (lax.div(x, 2) ^ jnp.where((h != lax.rem(x, 2)) & (core == 0), 1, 0)) == 1


def z_high(z, s, j):
    return (z + s * (((j - z) * s) & 3)) & 7 >= 4


def each_chunk(cols, body):
    n = CHUNK if cols % CHUNK == 0 else 128
    lax.fori_loop(0, cols // n, lambda i, c: (body(pl.multiple_of(i * n, n), n), c)[1], 0)


def give_z_kernel(start, src, out, buf, sem):
    z, x, core, s = place()
    copies = []
    for j in range(4):
        row = pl.multiple_of(jnp.where(z_high(z, s, j), 0, 64) + j * 16, 16)
        copies.append(pltpu.make_async_copy(src.at[pl.ds(row, 16), pl.ds(start, buf.shape[2])], buf.at[j], sem.at[j]))
    for copy in copies:
        copy.start()

    def body(j, first, n):
        here = (j, slice(None), pl.ds(first, n))
        out[here] = buf[here].astype(jnp.float32)

    for j, copy in enumerate(copies):
        copy.wait()
        each_chunk(buf.shape[2], functools.partial(body, j))


def give_x_kernel(start, src, out, buf, sem):
    z, x, core, s = place()
    copies = [
        pltpu.make_async_copy(src.at[pl.ds(j * 32, 32), pl.ds(start, buf.shape[2])], buf.at[j], sem.at[j]) for j in range(4)
    ]
    for copy in copies:
        copy.start()

    def body(j, first, n):
        high = jnp.broadcast_to(jnp.where(x_high(x, core), 1, 0), (8, n)) == 0
        for k in (2 * j, 2 * j + 1):
            rows = buf[k // 2, k % 2 * 16 : k % 2 * 16 + 16, pl.ds(first, n)].astype(jnp.float32)
            out[k, :, pl.ds(first, n)] = jnp.where(high, rows[8:], rows[:8])

    for j, copy in enumerate(copies):
        copy.wait()
        each_chunk(buf.shape[2], functools.partial(body, j))


def b_kernel(start, src, got, own, out, buf, sem):
    z, x, core, s = place()
    copies = []
    for j in range(4):
        row = pl.multiple_of(jnp.where(z_high(z, s, j), 64, 0) + j * 16, 16)
        copies.append(pltpu.make_async_copy(src.at[pl.ds(row, 16), pl.ds(start, buf.shape[2])], buf.at[j], sem.at[j]))
    for copy in copies:
        copy.start()

    def body(j, first, n):
        cols = pl.ds(first, n)
        high = jnp.broadcast_to(jnp.where(x_high(x, core), 1, 0), (8, n)) == 1
        rows = buf[j, :, cols].astype(jnp.float32) + got[j, :, cols]
        own[j * 8 : j * 8 + 8, cols] = jnp.where(high, rows[8:], rows[:8])
        out[j * 8 : j * 8 + 8, cols] = jnp.where(high, rows[:8], rows[8:])

    for j, copy in enumerate(copies):
        copy.wait()
        each_chunk(buf.shape[2], functools.partial(body, j))


def a_kernel(start, src, got, own, out, buf, sem):
    z, x, core, s = place()
    copies = [
        pltpu.make_async_copy(src.at[pl.ds(j * 32, 32), pl.ds(start, buf.shape[2])], buf.at[j], sem.at[j]) for j in range(4)
    ]
    for copy in copies:
        copy.start()
    for copy in copies:
        copy.wait()

    def body(first, n):
        cols = pl.ds(first, n)
        high = jnp.broadcast_to(jnp.where(x_high(x, core), 1, 0), (8, n)) == 1
        for j in range(4):
            there = []
            for zz in (j, j + 4):
                rows = buf[zz // 2, zz % 2 * 16 : zz % 2 * 16 + 16, cols].astype(jnp.float32)
                there.append(jnp.where(high, rows[8:], rows[:8]) + got[zz, :, cols])
            second = z_high(z, s, j)
            own[j * 8 : j * 8 + 8, cols] = jnp.where(second, there[1], there[0])
            out[j * 8 : j * 8 + 8, cols] = jnp.where(second, there[0], there[1])

    each_chunk(buf.shape[2], body)


def join_kernel(a, a_got, b, b_got, own, out):
    z, x, core, s = place()
    odd = lax.rem(x, 2) == 1

    def body(first, n):
        top = lax.broadcasted_iota(jnp.int32, (8, n), 0) < 4
        for kept, got, start in ((b, b_got, a.shape[1]), (a, a_got, 0)):
            for j in range(2):
                there = []
                for i in range(2):
                    here = (slice((2 * j + i) * 8, (2 * j + i) * 8 + 8), pl.ds(first, n))
                    rows = kept[here] + got[here]
                    turned = jnp.concatenate([rows[4:], rows[:4]], axis=0)
                    there.append((jnp.where(odd, turned, rows), jnp.where(odd, rows, turned)))
                here = (slice(j * 8, j * 8 + 8), pl.ds(start + first, n))
                own[here] = jnp.where(top, there[0][0], there[1][1])
                out[here] = jnp.where(top, there[0][1], there[1][0])

    each_chunk(a.shape[1], body)


def call(kernel, outs, scratch, *args, limit=LIMIT):
    vmem = pl.BlockSpec(memory_space=pltpu.VMEM)
    specs = [vmem] * len(args)
    if scratch:
        specs[0] = pl.BlockSpec(memory_space=pl.ANY)
    args = [v if spec is not vmem else pltpu.with_memory_space_constraint(v, pltpu.VMEM) for v, spec in zip(args, specs)]
    return pl.pallas_call(
        kernel,
        in_specs=specs,
        out_specs=[vmem] * len(outs),
        out_shape=[pltpu.VMEM(shape, jnp.float32) for shape in outs],
        scratch_shapes=[pltpu.VMEM(scratch, jnp.bfloat16), pltpu.SemaphoreType.DMA((scratch[0],))] if scratch else [],
        compiler_params=pltpu.CompilerParams(vmem_limit_bytes=limit),
        cost_estimate=pl.CostEstimate(flops=1024, bytes_accessed=1024, transcendentals=0),
    )(*args)


def last_step(own, z, s):
    out, last = [], None
    for k in ORDER:
        part = pick(own, (z + s * k) & 3, 0)
        out.append(part if last is None else after(part, last))
        last = out[-1]
    total = pick(own, z & 3, 0)
    for part, k in zip(out, ORDER):
        total = total + send_z_far(part, k)
    return total


def sum_parts(local):
    cols = local.shape[1]
    widths = [cols // 2 * w // UNIT for w in WIDTHS]
    a_at = [2 * sum(widths[:i]) for i in range(len(widths))]
    b_at = [a + w for a, w in zip(a_at, widths)]
    z, x, core, s = place()
    odd = lax.rem(x, 2) == 1

    later, a_got, b_got = local, [], []
    for a, b, n in zip(a_at, b_at, widths):
        (out,) = call(functools.partial(give_x_kernel, a), [(NZ, 8, n)], (4, 32, n), later, limit=None if later is local else LIMIT)
        a_got.append(send_x_first(out))
        later = after(local, out)
        (out,) = call(functools.partial(give_z_kernel, b), [(4, 16, n)], (4, 16, n), later)
        b_got.append(send_z_pair(out))
        later = after(local, out)
    a_own, b_own = [], []
    for i, n in enumerate(widths):
        own, out = call(functools.partial(a_kernel, a_at[i]), [(32, n)] * 2, (4, 32, n), later, a_got[i])
        a_own.append((own, send_z_pair(out)))
        later = after(local, out)
        own, out = call(functools.partial(b_kernel, b_at[i]), [(32, n)] * 2, (4, 16, n), later, b_got[i])
        b_own.append((own, send_x_first(out)))
        later = after(local, out)
    kept, last = [], None
    for (a, a_got), (b, b_got), n in zip(a_own, b_own, widths):
        own, out = call(join_kernel, [(16, 2 * n)] * 2, None, a if last is None else after(a, last), a_got, b, b_got)
        kept.append((own, send_x_second(out)))
        last = out
    done = []
    for own, got in kept:
        done.append((after(own, done[-1]) if done else own) + got)
    return last_step(jnp.concatenate(done, axis=1).reshape(4, 4, cols), z, s)


def sum_over_col(value):
    got = [lax.ppermute(value, "col", [(i, i ^ m) for i in range(NY)]) for m in COL_ORDER]
    return value + got[0] + got[1] + got[2]


def per_device(weight, momentum, grad_parts):
    gradient = sum_parts(grad_parts[0])
    squares = [jnp.sum(v * v, axis=1, keepdims=True) for v in (weight, gradient)]
    squares = sum_over_col(jnp.concatenate(squares, axis=1))
    weight_sq, grad_sq = squares[:, :1], squares[:, 1:]
    factor = jnp.minimum(1.0, clip_bound * jnp.sqrt(weight_sq) * lax.rsqrt(grad_sq + small_term))
    new_momentum = momentum_decay * momentum + factor * gradient
    return (weight - learn_rate * new_momentum, new_momentum)


def solution(mesh):
    in_specs = (P(("row", "dp"), "col"), P(("row", "dp"), "col"), P("dp", "row", "col"))
    out_specs = (P(("row", "dp"), "col"), P(("row", "dp"), "col"))
    return jax.shard_map(
        per_device, mesh=mesh, in_specs=in_specs, out_specs=out_specs, check_vma=False
    )
```
